32 devices in a mesh: section: 2 (over x), dp: 16 (over z, y, core).
Axes of the slice: x: 2, y: 2, z: 4, core: 2. Of those that a mesh axis runs over, the one named last changes fastest.
Arguments:
- tokens: bfloat16 [2, 16, 1024, 1280], P(None, 'dp'), may hold values from -6 to 6
- cotangent: bfloat16 [2, 16, 1024, 1280], P(None, 'dp'), may hold values from -6 to 6
- lengths: int32 [2, 16], P(None, 'dp'), may hold values from 30 to 1024, as said below
- predicted: int32 [2, 16, 1024], P(None, 'dp', 'section'), may hold values from 0 to 19
- truth: int32 [2, 16, 1024], P(None, 'dp', 'section'), may hold values from 0 to 19
- vec_d: bfloat16 [2, 3, 1280], P('section')
- w_in: bfloat16 [2, 1280, 640], P('section'), may hold values from -0.15625 to 0.15625
- vec_h: bfloat16 [2, 6, 640], P('section')
- w_conv: bfloat16 [2, 3200, 640], P('section'), may hold values from -0.109375 to 0.109375
- w_out: bfloat16 [2, 640, 1280], P('section'), may hold values from -0.5 to 0.5
Outputs:
- acts: bfloat16 [2, 2, 16, 1024, 1280], P('section', None, 'dp')
- in_grads: bfloat16 [2, 2, 16, 1024, 1280], P('section', None, 'dp')
- grad_vec_d: float32 [2, 3, 1280], P('section')
- grad_w_in: float32 [2, 1280, 640], P('section')
- grad_vec_h: float32 [2, 6, 640], P('section')
- grad_w_conv: float32 [2, 3200, 640], P('section')
- grad_w_out: float32 [2, 640, 1280], P('section')
- counts: int32 [2, 20], replicated
The draws below stay inside these ranges and needn't reach their ends.
Inputs may be any that keep to these rules, and one draw needn't show every extreme that they name: `lengths`: used rows of each sequence; some sequence has exactly 1024.
All inputs are finite; a program needn't handle non-finite values.
Results may differ from the reference program's by a relative error of at most 0.012.
Values may be sent and summed in bfloat16 or wider, within the bound.
No kernel may reach another device: no remote copies, remote signals or barrier semaphores. Data moves between devices by JAX's collectives and lax.ppermute only.
A program may use at most 256 MiB of HBM per device.

```python
import jax
import jax.numpy as jnp
from jax import lax

D = 1280
H = 640
KERNEL_TAPS = 5
FIRST_DILATION = 2
SECOND_DILATION = 128
LEN = 1024
MIN_LEN = 30
MICRO = 2
TYPES = 20
SEQS = 16


def draw_lengths(key, part):
    key = jax.random.fold_in(key, 7)
    first_key, second_key, third_key = jax.random.split(key, 3)
    span_rows = LEN - MIN_LEN + 1
    first_draw = jax.random.randint(first_key, (MICRO, SEQS), 0, span_rows)
    second_draw = jax.random.randint(second_key, (MICRO, SEQS), 0, span_rows)
    drawn = MIN_LEN + (first_draw + second_draw) // 2
    chosen = jax.random.randint(third_key, (), 0, MICRO * SEQS)
    flat_rows = jnp.where(jnp.arange(MICRO * SEQS) == chosen, LEN, drawn.reshape(-1))
    return flat_rows.reshape(MICRO, SEQS).astype(jnp.int32)


def draw_vec_d(key, part):
    key = jax.random.fold_in(key, 11)
    first_key, second_key = jax.random.split(key)
    gains = 1.0 + 0.3 * jax.random.uniform(first_key, (2, 3, D), jnp.float32, -1.0, 1.0)
    biases = 0.3 * jax.random.normal(second_key, (2, 3, D), jnp.float32)
    is_gain = jnp.arange(3) == 0
    return jnp.where(is_gain[None, :, None], gains, biases).astype(jnp.bfloat16)


def draw_vec_h(key, part):
    key = jax.random.fold_in(key, 13)
    first_key, second_key = jax.random.split(key)
    gains = 1.0 + 0.3 * jax.random.uniform(first_key, (2, 6, H), jnp.float32, -1.0, 1.0)
    biases = 0.3 * jax.random.normal(second_key, (2, 6, H), jnp.float32)
    row_ids = jnp.arange(6)
    is_gain = (row_ids == 1) | (row_ids == 4)
    return jnp.where(is_gain[None, :, None], gains, biases).astype(jnp.bfloat16)


def with_ends(entries, own_key, low, top_value):
    dims = entries.shape
    index_at = [jax.random.randint(jax.random.fold_in(own_key, axis), (), 0, dims[axis]) for axis in range(len(dims))]
    entries = entries.at[tuple(index_at)].set(low)
    longest = dims.index(max(dims))
    index_at[longest] = (index_at[longest] + 1) % dims[longest]
    return entries.at[tuple(index_at)].set(top_value)


def block_levels(rng, extent, cuts, low, largest):
    level = 1.0
    for axis_at, shards_of in cuts:
        steps = jax.random.uniform(jax.random.fold_in(jax.random.fold_in(rng, 6), axis_at), (shards_of,), jnp.float32, low / len(cuts), largest / len(cuts))
        level = level * jnp.repeat(jnp.exp(steps), extent[axis_at] // shards_of).reshape((-1,) + (1,) * (len(extent) - 1 - axis_at))
    return level


def normal_values(rng, dims, deviation, bound, cuts=(), kind=jnp.bfloat16):
    values = deviation * jax.random.normal(rng, dims, jnp.float32)
    if cuts:
        values = values * block_levels(rng, dims, cuts, -0.22, 0.18)
    return jnp.clip(values, -bound, bound).astype(kind)


def setup_inputs(seed: int = 0) -> dict:
    key_of = jax.random.split(jax.random.key(seed), 11)
    tokens = normal_values(key_of[0], (MICRO, SEQS, LEN, D), 1.0, 6.0, ((1, 16),))
    cotangent = normal_values(key_of[1], (MICRO, SEQS, LEN, D), 1.0, 6.0, ((1, 16),))
    lengths = draw_lengths(jax.random.fold_in(key_of[10], 71), 0)
    predicted = with_ends(jax.random.randint(key_of[3], (MICRO, SEQS, LEN), 0, TYPES), jax.random.fold_in(key_of[3], 1), 0, TYPES - 1).astype(jnp.int32)
    truth = with_ends(jax.random.randint(key_of[4], (MICRO, SEQS, LEN), 0, TYPES), jax.random.fold_in(key_of[4], 1), 0, TYPES - 1).astype(jnp.int32)
    vec_d = draw_vec_d(jax.random.fold_in(key_of[10], 71), 0)
    w_in = normal_values(key_of[6], (2, D, H), D ** -0.5, 0.15625, ((0, 2),))
    vec_h = draw_vec_h(jax.random.fold_in(key_of[10], 71), 0)
    w_conv = normal_values(key_of[8], (2, KERNEL_TAPS * H, H), (KERNEL_TAPS * H) ** -0.5, 0.109375, ((0, 2),))
    w_out = normal_values(key_of[9], (2, H, D), (H // 4) ** -0.5, 0.5, ((0, 2),))
    return {"tokens": tokens, "cotangent": cotangent, "lengths": lengths, "predicted": predicted, "truth": truth, "vec_d": vec_d, "w_in": w_in, "vec_h": vec_h, "w_conv": w_conv, "w_out": w_out}


EPSILON = 1e-05

@jax.custom_vjp
def low(v):
    return lax.optimization_barrier(v.astype(jnp.bfloat16)).astype(jnp.float32)

@jax.custom_vjp
def low_back(v):
    return v

def low_keep(v):
    return (low(v), None)

def low_pass(kept, grad):
    return (grad,)

def back_keep(v):
    return (v, None)

def back_low(kept, grad):
    return (low(grad),)
low.defvjp(low_keep, low_pass)
low_back.defvjp(back_keep, back_low)

def norm_gelu(values, gain_row, bias_row):
    row_mean = lax.optimization_barrier(jnp.mean(values, -1, keepdims=True))
    centred = values - row_mean
    spread = lax.optimization_barrier(jnp.mean(centred * centred, -1, keepdims=True))
    return jax.nn.gelu(centred * lax.rsqrt(spread + EPSILON) * gain_row + bias_row)

def matmul(left, right):
    return jnp.dot(left, right, precision=lax.Precision.HIGHEST)

def tapped(second_act, tap_spacing):
    receptive_rows = KERNEL_TAPS // 2 * tap_spacing
    padded = jnp.pad(second_act, ((0, 0), (receptive_rows, receptive_rows), (0, 0)))
    return jnp.concatenate([padded[:, tap_no * tap_spacing:tap_no * tap_spacing + LEN, :] for tap_no in range(KERNEL_TAPS)], -1)

def block_apply(block_input, params, valid_row_mask, tap_spacing):
    vec_dw, vec_hw, w_inw, w_convw, w_outw = params
    first_act = low(norm_gelu(block_input, vec_dw[0], vec_dw[1]))
    inner_pre = low_back(matmul(first_act, w_inw) + vec_hw[0])
    second_act = low(norm_gelu(inner_pre, vec_hw[1], vec_hw[2]) * valid_row_mask)
    conv_pre = low_back(matmul(tapped(second_act, tap_spacing), w_convw) + vec_hw[3])
    third_act = low(norm_gelu(conv_pre, vec_hw[4], vec_hw[5]))
    branch = low_back(matmul(third_act, w_outw) + vec_dw[2])
    return block_input + branch * valid_row_mask

def reference(tokens, cotangent, lengths, predicted, truth, vec_d, w_in, vec_h, w_conv, w_out):
    arrays = (vec_d, vec_h, w_in, w_conv, w_out)
    params = [tuple((array.astype(jnp.float32)[which] for array in arrays)) for which in range(2)]
    places = jnp.arange(LEN, dtype=jnp.int32)

    def network(block_input, first_block_params, second_block_params, offset_zero, valid_row_mask):
        lower_output = block_apply(block_input, first_block_params, valid_row_mask, FIRST_DILATION)
        middle_output = low_back(low(lower_output)) + offset_zero
        return (middle_output, block_apply(middle_output, second_block_params, valid_row_mask, SECOND_DILATION))

    def per_sequence(carry, seq_index):
        block_input = lax.dynamic_index_in_dim(tokens, seq_index, 1, keepdims=False).astype(jnp.float32)
        cot_block = lax.dynamic_index_in_dim(cotangent, seq_index, 1, keepdims=False).astype(jnp.float32)
        seq_lengths = lax.dynamic_index_in_dim(lengths, seq_index, 1, keepdims=False)
        valid_row_mask = (places[None, :] < seq_lengths[:, None]).astype(jnp.float32)[:, :, None]
        offset_zero = jnp.zeros_like(block_input)
        (middle_output, result), pull = jax.vjp(lambda inputs, former, latter, offset: network(inputs, former, latter, offset, valid_row_mask), block_input, params[0], params[1], offset_zero)
        grad_in, grad_first, grad_second, grad_middle = pull((jnp.zeros_like(middle_output), cot_block))
        carry = jax.tree.map(lambda former, latter: former + latter, carry, (grad_first, grad_second))
        return (carry, (middle_output.astype(jnp.bfloat16), result.astype(jnp.bfloat16), grad_in.astype(jnp.bfloat16), grad_middle.astype(jnp.bfloat16)))
    start = jax.tree.map(jnp.zeros_like, (params[0], params[1]))
    summed, (middles, results, grads_in, grads_middle) = lax.scan(per_sequence, start, jnp.arange(SEQS, dtype=jnp.int32))
    acts = jnp.stack([jnp.swapaxes(middles, 0, 1), jnp.swapaxes(results, 0, 1)])
    in_grads = jnp.stack([jnp.swapaxes(grads_in, 0, 1), jnp.swapaxes(grads_middle, 0, 1)])
    stacked = [jnp.stack([summed[0][which], summed[1][which]]) for which in range(5)]
    live_rows = places[None, None, :] < lengths[:, :, None]
    right_rows = live_rows & (predicted == truth)
    kind_hits = truth[..., None] == jnp.arange(TYPES, dtype=jnp.int32)
    correct = lax.optimization_barrier(jnp.sum((kind_hits & right_rows[..., None]).astype(jnp.int32), (0, 1, 2)))
    totals = lax.optimization_barrier(jnp.sum((kind_hits & live_rows[..., None]).astype(jnp.int32), (0, 1, 2)))
    counts = jnp.stack([correct, totals]).astype(jnp.int32)
    return (acts, in_grads, stacked[0], stacked[2], stacked[1], stacked[3], stacked[4], counts)
```

```python
import functools
import math

import jax
import jax.numpy as jnp
from jax import lax
from jax.experimental import pallas as pl
from jax.experimental.pallas import tpu as pltpu
from jax.sharding import PartitionSpec as P

KERNEL_TAPS = 5
FIRST_DILATION = 2
SECOND_DILATION = 128
TYPES = 20
EPSILON = 1e-05

TILE = 256
WIDE_CHUNK = 16
CHUNK = 32
HALO = 256
VMEM_LIMIT = 63 * 1024 * 1024

GELU_K = math.sqrt(2.0 / math.pi)
GELU_A = 0.044715

BF16 = jnp.bfloat16
F32 = jnp.float32


def dot_nn(left, right):
    return jnp.dot(left, right, preferred_element_type=F32)


def dot_nt(left, right):
    return lax.dot_general(left, right, (((1,), (1,)), ((), ())), preferred_element_type=F32)


def dot_tn(left, right):
    return lax.dot_general(left, right, (((0,), (0,)), ((), ())), preferred_element_type=F32)


def normed(values):
    centred = values - jnp.mean(values, -1, keepdims=True)
    rstd = lax.rsqrt(jnp.mean(centred * centred, -1, keepdims=True) + EPSILON)
    return centred * rstd, rstd


def gelu_parts(n):
    inner = (n * n) * (GELU_K * GELU_A) + GELU_K
    half = 0.5 * jnp.tanh(n * inner) + 0.5
    act = n * half
    slope = half + act * (1.0 - half) * (6.0 * inner - 4.0 * GELU_K)
    return act, slope


def gelu_only(n):
    inner = (n * n) * (GELU_K * GELU_A) + GELU_K
    return n * (0.5 * jnp.tanh(n * inner) + 0.5)


def folded(values):
    rows, width = values.shape
    return jnp.sum(values.reshape(rows // 8, 8, width), 0)


def norm_back(grad, hat, slope, gain, rstd):
    gn = grad * slope
    gn_hat = gn * hat
    gg = gn * gain
    gg_mean = jnp.mean(gg, -1, keepdims=True)
    gg_hat_mean = jnp.mean(gg * hat, -1, keepdims=True)
    return (gg - gg_mean - hat * gg_hat_mean) * rstd, folded(gn_hat), folded(gn)


def tile_rows(tile_no):
    return pl.multiple_of(tile_no * TILE, TILE)


def gather_taps(padded, stack, start, spacing, sign, width):
    if spacing % 16 == 0:
        for tap in range(KERNEL_TAPS):
            shift = sign * (tap - KERNEL_TAPS // 2) * spacing
            rows = pl.ds(pl.multiple_of(start + HALO + shift, 16), TILE)
            stack[:, tap * width : (tap + 1) * width] = padded[rows, :]
    else:
        edge = 16
        part = 128
        for piece in range(width // part):
            columns = slice(piece * part, (piece + 1) * part)
            window = padded[pl.ds(pl.multiple_of(start + HALO - edge, 16), TILE + 2 * edge), columns]
            window = window.astype(F32)
            for tap in range(KERNEL_TAPS):
                shift = sign * (tap - KERNEL_TAPS // 2) * spacing
                moved = window if shift == 0 else pltpu.roll(window, (-shift) % (TILE + 2 * edge), 0)
                stack[:, tap * width + piece * part : tap * width + (piece + 1) * part] = moved[
                    edge : edge + TILE
                ].astype(BF16)


def row_live(start, length, rows):
    places = lax.broadcasted_iota(jnp.int32, (rows, 1), 0) + start
    return (places < length).astype(F32)


def each_chunk(start, chunk, body):
    for at in range(0, TILE, chunk):
        body(pl.ds(at, chunk), pl.ds(start + at, chunk), start + at)


def forward_first(tile_no, length, entry, vec_d, vec_h, w_in, tile_d, tile_h, second, hat2, slope2, rstds):
    start = tile_rows(tile_no)

    def first_norm(local_rows, rows, at):
        hat, _ = normed(entry[rows, :].astype(F32))
        tile_d[local_rows, :] = gelu_only(hat * vec_d[0:1, :] + vec_d[1:2, :]).astype(BF16)

    def second_norm(local_rows, rows, at):
        hat, rstd = normed(tile_h[local_rows, :] + vec_h[0:1, :])
        act, slope = gelu_parts(hat * vec_h[1:2, :] + vec_h[2:3, :])
        second[pl.ds(at + HALO, CHUNK), :] = (act * row_live(at, length, CHUNK)).astype(BF16)
        if hat2 is not None:
            hat2[rows, :] = hat.astype(BF16)
            slope2[rows, :] = slope.astype(BF16)
            rstds[rows, 0:1] = rstd

    each_chunk(start, WIDE_CHUNK, first_norm)
    tile_h[...] = dot_nn(tile_d[...], w_in[...])
    each_chunk(start, CHUNK, second_norm)


def forward_second(tile_no, length, spacing, entry, vec_d, vec_h, w_conv, w_out, stack, tile_h, tile_f, second, hat3, slope3, third, rstds, act_out):
    start = tile_rows(tile_no)

    def third_norm(local_rows, rows, at):
        hat, rstd = normed(tile_h[local_rows, :] + vec_h[3:4, :])
        act, slope = gelu_parts(hat * vec_h[4:5, :] + vec_h[5:6, :])
        third[rows, :] = (act * row_live(at, length, CHUNK)).astype(BF16)
        if hat3 is not None:
            hat3[rows, :] = hat.astype(BF16)
            slope3[rows, :] = slope.astype(BF16)
            rstds[rows, 1:2] = rstd

    def result(local_rows, rows, at):
        branch = (tile_f[local_rows, :] + vec_d[2:3, :]) * row_live(at, length, WIDE_CHUNK)
        act_out[rows, :] = (entry[rows, :].astype(F32) + branch).astype(BF16)

    gather_taps(second, stack, start, spacing, 1, third.shape[-1])
    tile_h[...] = dot_nn(stack[...], w_conv[...])
    each_chunk(start, CHUNK, third_norm)
    if act_out is not None:
        tile_f[...] = dot_nn(third[pl.ds(start, TILE), :], w_out[...])
        each_chunk(start, WIDE_CHUNK, result)


def backward_first(tile_no, length, grad_out, vec_h, wout_t, tile_h, third, hat3, slope3, rstds, grad_conv, sum_d, sum_h, acc_out):
    start = tile_rows(tile_no)

    def third_back(local_rows, rows, at):
        live = row_live(at, length, CHUNK)
        grad, gain_sum, bias_sum = norm_back(
            tile_h[local_rows, :] * live,
            hat3[rows, :].astype(F32),
            slope3[rows, :].astype(F32),
            vec_h[4:5, :],
            rstds[rows, 1:2],
        )
        grad_low = grad.astype(BF16)
        grad_conv[pl.ds(at + HALO, CHUNK), :] = grad_low
        if sum_h is not None:
            sum_h[3] += folded(grad_low.astype(F32))
            sum_h[4] += gain_sum
            sum_h[5] += bias_sum
            sum_d[2] += folded(grad_out[rows, :].astype(F32) * live)

    rows = pl.ds(start, TILE)
    tile_h[...] = dot_nn(grad_out[rows, :], wout_t[...])
    if acc_out is not None:
        acc_out[...] += dot_tn(third[rows, :], grad_out[rows, :])
    each_chunk(start, CHUNK, third_back)


def backward_second(tile_no, length, spacing, entry, grad_out, vec_d, vec_h, w_in, wconv_t, tile_d, tile_h, tile_f, tile_g, stack, second, hat2, slope2, rstds, grad_conv, sum_d, sum_h, acc_in, acc_conv, grad_in):
    start = tile_rows(tile_no)
    inner = w_in.shape[1]

    def second_back(local_rows, rows, at):
        grad, gain_sum, bias_sum = norm_back(
            tile_h[local_rows, :] * row_live(at, length, CHUNK),
            hat2[rows, :].astype(F32),
            slope2[rows, :].astype(F32),
            vec_h[1:2, :],
            rstds[rows, 0:1],
        )
        grad_low = grad.astype(BF16)
        tile_g[local_rows, :] = grad_low
        if sum_h is not None:
            sum_h[0] += folded(grad_low.astype(F32))
            sum_h[1] += gain_sum
            sum_h[2] += bias_sum

    def first_back(local_rows, rows, at):
        hat, rstd = normed(entry[rows, :].astype(F32))
        act, slope = gelu_parts(hat * vec_d[0:1, :] + vec_d[1:2, :])
        if acc_in is not None:
            tile_d[local_rows, :] = act.astype(BF16)
        grad, gain_sum, bias_sum = norm_back(tile_f[local_rows, :], hat, slope, vec_d[0:1, :], rstd)
        grad_in[rows, :] = (grad_out[rows, :].astype(F32) + grad).astype(BF16)
        if sum_d is not None:
            sum_d[0] += gain_sum
            sum_d[1] += bias_sum

    gather_taps(grad_conv, stack, start, spacing, -1, inner)
    tile_h[...] = dot_nn(stack[...], wconv_t[...])
    if acc_conv is not None:
        rows = pl.ds(pl.multiple_of(start + HALO, HALO), TILE)
        for tap in range(KERNEL_TAPS):
            block = slice(tap * inner, (tap + 1) * inner)
            acc_conv[block, :] += dot_tn(second[rows, :], stack[:, block])
    each_chunk(start, CHUNK, second_back)
    tile_f[...] = dot_nt(tile_g[...], w_in[...])
    each_chunk(start, WIDE_CHUNK, first_back)
    if acc_in is not None:
        acc_in[...] += dot_tn(tile_d[...], tile_g[...])


def loop(low, high, body):
    def step(tile_no, carry):
        body(tile_no)
        return carry

    lax.fori_loop(low, high, step, 0)


def pass_through(source, target, tiles, total_tiles):
    def step(tile_no):
        rows = pl.ds(tile_rows(tile_no), TILE)
        target[rows, :] = source[rows, :]

    loop(tiles, total_tiles, step)


def tiles_of(length):
    return lax.div(length + (TILE - 1), TILE)


WIN_PART, WCONV_PART, WOUT_PART, VEC_ROWS = 160, 400, 80, 32
TAIL_ROWS = 128


class Copies:
    def __init__(self, sems, first=0):
        self.sems, self.next, self.open = sems, first, []

    def start(self, source, target):
        copy = pltpu.make_async_copy(source, target, self.sems.at[self.next])
        self.next += 1
        copy.start()
        self.open.append(copy)
        return copy

    def wait(self):
        for copy in self.open:
            copy.wait()
        self.open = []


def zero_rows(ref):
    step = 128

    def body(i):
        ref[pl.ds(pl.multiple_of(i * step, step), step), :] = jnp.zeros((step, ref.shape[1]), ref.dtype)

    loop(0, ref.shape[0] // step, body)


FIRST_SEM, LATER_SEM, OUT_SEM, SLOT_SEM, N_SEMS = 8, 33, 41, 44, 64


def weight_copies(sems, unit, source, target):
    vecs, win_v, wconv_v, wout_v = target
    now, later = [], []
    if len(source) == 4:
        from_vecs, from_in, from_conv, from_out = source
        now += [(from_vecs, vecs), (from_in, win_v), (from_out, wout_v)]
        later.append((from_conv, wconv_v))
    else:
        width = win_v.shape[1]
        a, b, c = WIN_PART, WIN_PART + WOUT_PART, WIN_PART + 2 * WOUT_PART
        for j in range(8):
            which = unit ^ j
            first, second = source[j], source[8 + j]
            at_in = pl.ds(pl.multiple_of(which * WIN_PART, WIN_PART), WIN_PART)
            at_conv = pl.ds(pl.multiple_of(which * WCONV_PART, WCONV_PART), WCONV_PART)
            at_out = pl.ds(pl.multiple_of(which * WOUT_PART, WOUT_PART), WOUT_PART)
            now.append((first.at[0:a], win_v.at[at_in]))
            now.append((first.at[a:b], wout_v.at[at_out, 0:width]))
            now.append((first.at[b:c], wout_v.at[at_out, width : 2 * width]))
            if j == 0:
                now.append((first.at[c : c + VEC_ROWS], vecs))
            later.append((second, wconv_v.at[at_conv]))
    return (
        [pltpu.make_async_copy(src, dst, sems.at[FIRST_SEM + i]) for i, (src, dst) in enumerate(now)],
        [pltpu.make_async_copy(src, dst, sems.at[LATER_SEM + i]) for i, (src, dst) in enumerate(later)],
    )


def start_all(copies):
    for copy in copies:
        copy.start()


def wait_all(copies):
    for copy in copies:
        copy.wait()


def transpose_blocks(source, target, blocks=1):
    rows, columns = source.shape[0] // blocks, source.shape[1]

    def block(k):
        for at in range(0, columns, TAIL_ROWS):
            values = source[pl.ds(pl.multiple_of(k * rows, rows), rows), at : at + TAIL_ROWS]
            target[pl.ds(pl.multiple_of(k * columns + at, TAIL_ROWS), TAIL_ROWS), :] = values.T

    loop(0, blocks, block)


def spread_vecs(vecs, vd, vh):
    rows = vecs[...].astype(F32)
    width = rows.shape[1]
    vd[:, 0:width] = rows[0:8]
    vd[:, width : 2 * width] = rows[8:16]
    vh[...] = rows[16:24]


SCALARS = pl.BlockSpec(memory_space=pltpu.SMEM)
ANYWHERE = pl.BlockSpec(memory_space=pl.ANY)
N_SAVED = 7


def forward_kernel(spacing, from_own, save, parts, n_weights, n_kept, lens, flags, entry, *refs):
    weights, refs = refs[:n_weights], refs[n_weights + n_kept :]
    act_out, refs = refs[0], refs[1:]
    if save:
        saved_out, refs = refs[:N_SAVED], refs[N_SAVED:]
    (vecs, win_v, wconv_v, wout_v, vd, vh, entry_v, act_v, tile_d, tile_h, tile_f, stack, sems), saved = refs[:13], refs[13:]
    length_rows = entry.shape[1]
    total_tiles = length_rows // TILE

    @pl.when(flags[0] == 1)
    def _():
        low, high = parts

        def arrival(m):
            return pltpu.make_async_copy(entry.at[m], entry_v.at[m - low], sems.at[m])

        def departures(m):
            copies = [(act_v.at[m - low], act_out.at[m])]
            if save:
                for ref, out in zip(saved, saved_out):
                    source = ref.at[m - low]
                    if ref is saved[0]:
                        source = source.at[HALO : HALO + length_rows]
                    copies.append((source, out.at[m]))
            return [
                pltpu.make_async_copy(src, dst, sems.at[OUT_SEM + len(copies) * (m - low) + i])
                for i, (src, dst) in enumerate(copies)
            ]

        now, later = weight_copies(sems, flags[1], weights, (vecs, win_v, wconv_v, wout_v))
        arrival(low).start()
        start_all(now)
        start_all(later)
        wait_all(now)
        spread_vecs(vecs, vd, vh)

        def one(m):
            arrival(m).wait()
            x, act = entry_v.at[m - low], act_v.at[m - low]
            if save:
                second, hat2, slope2, hat3, slope3, third, rstds = (ref.at[m - low] for ref in saved)
            else:
                second, third = saved
                hat2 = slope2 = hat3 = slope3 = rstds = None
            zero_rows(second)
            length = lens[m]
            tiles = tiles_of(length)
            loop(0, tiles, lambda t: forward_first(t, length, x, vd, vh, win_v, tile_d, tile_h, second, hat2, slope2, rstds))

            @pl.when(m == low)
            def _():
                wait_all(later)
                for other in range(low + 1, high):
                    arrival(other).start()

            loop(0, tiles, lambda t: forward_second(t, length, spacing, x, vd, vh, wconv_v, wout_v, stack, tile_h, tile_f, second, hat3, slope3, third, rstds, act))
            pass_through(x, act, tiles, total_tiles)
            start_all(departures(m))

        loop(low, high, one)

        def leave(m):
            wait_all(departures(m))

        loop(low, high, leave)


def start_sums(sum_d, sum_h, accs):
    for ref in accs:
        zero_rows(ref)
    sum_d[...] = jnp.zeros_like(sum_d)
    sum_h[...] = jnp.zeros_like(sum_h)


SLOTS = 4
CHAIN_ROWS = 12 * TAIL_ROWS


class Flush:
    def __init__(self, accs, core, targets, stage, sems):
        self.acc_in, self.acc_conv, self.acc_out = accs
        self.core, self.targets, self.stage, self.sems = core, targets, stage, sems
        self.rows, self.width = stage.shape[1:]
        self.count_in, self.count_conv, self.count_out = (acc.shape[0] // self.rows for acc in accs)

    def copy_of(self, slot, target, at):
        return pltpu.make_async_copy(self.stage.at[slot], target.at[pl.ds(at, self.rows), :], self.sems.at[SLOT_SEM + slot])

    def send(self, number, block, values):
        slot = lax.rem(number, SLOTS)

        @pl.when(number >= SLOTS)
        def _():
            self.copy_of(slot, self.targets[0], 0).wait()

        self.stage[slot] = values.astype(BF16)
        chain = self.targets[0].shape[0] // self.rows
        half = chain + self.targets[1].shape[0] // self.rows
        is_second = (block >= half).astype(jnp.int32)
        in_half = block - is_second * half
        other = (is_second != self.core).astype(jnp.int32)
        for which, target in enumerate(self.targets):
            later = which % 2
            fits = (in_half >= chain) if later else (in_half < chain)

            @pl.when(fits & (other == which // 2))
            def _():
                self.copy_of(slot, target, pl.multiple_of((in_half - later * chain) * self.rows, self.rows)).start()

    def blocks(self, acc, columns, number, block):
        def body(i):
            values = acc[pl.ds(pl.multiple_of(i * self.rows, self.rows), self.rows), columns]
            self.send(number + i, block + i, values)

        loop(0, acc.shape[0] // self.rows, body)

    def out(self):
        at = 1 + self.count_in + self.count_conv
        self.blocks(self.acc_out, slice(0, self.width), 0, at)
        self.blocks(self.acc_out, slice(self.width, 2 * self.width), self.count_out, at + self.count_out)

    def rest(self, sum_d, sum_h, digits, tail):
        sent, width = 2 * self.count_out, self.width
        self.blocks(self.acc_conv, slice(0, width), sent, 1 + self.count_in)
        self.blocks(self.acc_in, slice(0, width), sent + self.count_conv, 1)
        tail[...] = jnp.zeros_like(tail)
        for i in range(3):
            row = jnp.sum(sum_d[i], 0, keepdims=True)
            tail[i : i + 1, :] = row[:, 0:width]
            tail[8 + i : 9 + i, :] = row[:, width : 2 * width]
        for i in range(6):
            tail[16 + i : 17 + i, :] = jnp.sum(sum_h[i], 0, keepdims=True)
        tail[32 : 32 + digits.shape[0], :] = digits[...]
        self.send(jnp.int32(sent + self.count_conv + self.count_in), jnp.int32(0), tail[...])
        for slot in range(SLOTS):
            self.copy_of(slot, self.targets[0], 0).wait()


def middle_kernel(spacing, parts, n_other, lens, flags, entry, entry_upper, cot, digits, *refs):
    own, refs = refs[:4], refs[4:]
    other, refs = refs[:n_other], refs[n_other:]
    act_out, grad_in_out, *targets = refs[:6]
    refs = refs[6:]
    (vecs, win_v, wconv_v, wout_v, vd, vh, wconv_t, wout_t, entry_v, cot_v, out_v, second, grad_conv,
     hat2, slope2, hat3, slope3, third, rstds, tile_d, tile_h, tile_f, tile_g, stack,
     acc_in, acc_conv, acc_out, sum_d, sum_h, stage, sems) = refs
    total_tiles = entry_v.shape[1] // TILE
    weigh = flags[0]
    accs = (acc_in, acc_conv, acc_out)
    target = (vecs, win_v, wconv_v, wout_v)
    flush = Flush(accs, flags[2], targets, stage, sems)

    def cot_arrival(m):
        return pltpu.make_async_copy(cot.at[m], cot_v.at[m], sems.at[m])

    def entry_arrival(m, source=entry):
        return pltpu.make_async_copy(source.at[m], entry_v.at[m], sems.at[parts + m])

    def start_entry(m):
        pl.when(weigh == 1)(lambda: entry_arrival(m, entry_upper).start())
        pl.when(weigh == 0)(lambda: entry_arrival(m).start())

    def act_departure(m):
        return pltpu.make_async_copy(out_v, act_out.at[m], sems.at[OUT_SEM])

    def grad_departure(m):
        return pltpu.make_async_copy(out_v, grad_in_out.at[m], sems.at[OUT_SEM + 1])

    def with_weights(do):
        pl.when(weigh == 1)(lambda: do(*weight_copies(sems, flags[1], own, target)))
        pl.when(weigh == 0)(lambda: do(*weight_copies(sems, flags[1], other, target)))

    def start_weights(now, later):
        start_all(now)
        start_all(later)

    start_entry(0)
    with_weights(start_weights)
    cot_arrival(0).start()

    @pl.when(weigh == 1)
    def _():
        start_sums(sum_d, sum_h, accs)

    with_weights(lambda now, later: wait_all(now))
    spread_vecs(vecs, vd, vh)

    def one(m):
        entry_arrival(m).wait()
        x, gy = entry_v.at[m], cot_v.at[m]
        length = lens[m]
        tiles = tiles_of(length)
        zero_rows(second)
        zero_rows(grad_conv)
        loop(0, tiles, lambda t: forward_first(t, length, x, vd, vh, win_v, tile_d, tile_h, second, hat2, slope2, rstds))

        @pl.when(m == 0)
        def _():
            with_weights(lambda now, later: wait_all(later))
            for later_part in range(1, parts):
                start_entry(later_part)
                cot_arrival(later_part).start()

        def forward_rest(act):
            loop(0, tiles, lambda t: forward_second(t, length, spacing, x, vd, vh, wconv_v, wout_v, stack, tile_h, tile_f, second, hat3, slope3, third, rstds, act))

        @pl.when(weigh == 1)
        def _():
            pl.when(m > 0)(lambda: grad_departure(m - 1).wait())
            forward_rest(out_v)
            pass_through(x, out_v, tiles, total_tiles)
            act_departure(m).start()

        pl.when(weigh == 0)(lambda: forward_rest(None))

        @pl.when(m == 0)
        def _():
            transpose_blocks(wout_v, wout_t)
            transpose_blocks(wconv_v, wconv_t, KERNEL_TAPS)

        cot_arrival(m).wait()

        def back_first(sum_d, sum_h, acc_out):
            loop(0, tiles, lambda t: backward_first(t, length, gy, vh, wout_t, tile_h, third, hat3, slope3, rstds, grad_conv, sum_d, sum_h, acc_out))

        def back_second(sum_d, sum_h, acc_in, acc_conv):
            loop(0, tiles, lambda t: backward_second(t, length, spacing, x, gy, vd, vh, win_v, wconv_t, tile_d, tile_h, tile_f, tile_g, stack, second, hat2, slope2, rstds, grad_conv, sum_d, sum_h, acc_in, acc_conv, out_v))

        @pl.when(weigh == 1)
        def _():
            back_first(sum_d, sum_h, acc_out)
            pl.when(m == parts - 1)(flush.out)
            act_departure(m).wait()
            back_second(sum_d, sum_h, acc_in, acc_conv)

        @pl.when(weigh == 0)
        def _():
            back_first(None, None, None)
            pl.when(m > 0)(lambda: grad_departure(m - 1).wait())
            back_second(None, None, None, None)

        pass_through(gy, out_v, tiles, total_tiles)
        grad_departure(m).start()

    loop(0, parts, one)

    @pl.when(weigh == 1)
    def _():
        flush.rest(sum_d, sum_h, digits, tile_h.at[0:TAIL_ROWS])

    grad_departure(parts - 1).wait()


def first_back_kernel(spacing, parts, lens, flags, entry, grad_out, digits, *refs):
    weights, refs = refs[:4], refs[4:]
    saved_in, refs = refs[:N_SAVED], refs[N_SAVED:]
    refs = refs[4:]
    grad_in_out, *targets = refs[:5]
    refs = refs[5:]
    (vecs, win_v, wconv_v, wout_v, vd, vh, wconv_t, wout_t, entry_v, gy_v, grad_v, grad_conv,
     tile_d, tile_h, tile_f, tile_g, stack, acc_in, acc_conv, acc_out, sum_d, sum_h, stage,
     second, hat2, slope2, hat3, slope3, third, rstds, sems) = refs
    saved = (second, hat2, slope2, hat3, slope3, third, rstds)
    length_rows = entry.shape[1]
    total_tiles = length_rows // TILE
    accs = (acc_in, acc_conv, acc_out)

    @pl.when(flags[0] == 1)
    def _():
        def gy_arrival(m):
            return pltpu.make_async_copy(grad_out.at[m], gy_v.at[m], sems.at[m])

        def entry_arrival(m):
            return pltpu.make_async_copy(entry.at[m], entry_v.at[m], sems.at[parts + m])

        def saved_arrivals(m, names):
            places = {"second": 0, "hat2": 1, "slope2": 2, "hat3": 3, "slope3": 4, "third": 5}
            copies = []
            for name in names:
                i = places[name]
                dst = saved[i].at[HALO : HALO + length_rows] if name == "second" else saved[i]
                copies.append(pltpu.make_async_copy(saved_in[i].at[m], dst, sems.at[FIRST_SEM + 8 + i]))
            return copies

        for_first, for_second = ("hat3", "slope3", "third"), ("hat2", "slope2", "second")
        rstds_arrival = pltpu.make_async_copy(saved_in[6], rstds, sems.at[FIRST_SEM + 14])
        (vecs_in, win_in, wout_in), (wconv_in,) = weight_copies(sems, 0, weights, (vecs, win_v, wconv_v, wout_v))
        start_all([vecs_in, wout_in, gy_arrival(0), rstds_arrival] + saved_arrivals(0, for_first))
        start_all([wconv_in, win_in] + saved_arrivals(0, for_second) + [entry_arrival(0)])
        start_sums(sum_d, sum_h, accs)
        flush = Flush(accs, flags[2], targets, stage, sems)
        wait_all([vecs_in, wout_in])
        spread_vecs(vecs, vd, vh)
        transpose_blocks(wout_v, wout_t)
        rstds_arrival.wait()

        def grad_departure(m):
            return pltpu.make_async_copy(grad_v, grad_in_out.at[m], sems.at[OUT_SEM])

        def one(m):
            gy_arrival(m).wait()
            wait_all(saved_arrivals(m, for_first))
            x, gy, own_rstds = entry_v.at[m], gy_v.at[m], rstds.at[m]
            length = lens[m]
            tiles = tiles_of(length)
            zero_rows(grad_conv)
            loop(0, tiles, lambda t: backward_first(t, length, gy, vh, wout_t, tile_h, third, hat3, slope3, own_rstds, grad_conv, sum_d, sum_h, acc_out))

            @pl.when(m < parts - 1)
            def _():
                start_all([gy_arrival(m + 1), entry_arrival(m + 1)] + saved_arrivals(m + 1, for_first))

            pl.when(m == parts - 1)(flush.out)

            @pl.when(m == 0)
            def _():
                wait_all([wconv_in, win_in])
                transpose_blocks(wconv_v, wconv_t, KERNEL_TAPS)

            entry_arrival(m).wait()
            wait_all(saved_arrivals(m, for_second))
            pl.when(m > 0)(lambda: grad_departure(m - 1).wait())
            loop(0, tiles, lambda t: backward_second(t, length, spacing, x, gy, vd, vh, win_v, wconv_t, tile_d, tile_h, tile_f, tile_g, stack, second, hat2, slope2, own_rstds, grad_conv, sum_d, sum_h, acc_in, acc_conv, grad_v))
            pass_through(gy, grad_v, tiles, total_tiles)
            grad_departure(m).start()

            @pl.when(m < parts - 1)
            def _():
                start_all(saved_arrivals(m + 1, for_second))

        loop(0, parts, one)
        flush.rest(sum_d, sum_h, digits, tile_h.at[0:TAIL_ROWS])
        grad_departure(parts - 1).wait()


def weight_scratch(width, inner):
    return [
        pltpu.VMEM((VEC_ROWS, inner), BF16),
        pltpu.VMEM((width, inner), BF16),
        pltpu.VMEM((KERNEL_TAPS * inner, inner), BF16),
        pltpu.VMEM((inner, width), BF16),
        pltpu.VMEM((8, width), F32),
        pltpu.VMEM((8, inner), F32),
    ]


def transposed_scratch(width, inner):
    return [pltpu.VMEM((KERNEL_TAPS * inner, inner), BF16), pltpu.VMEM((width, inner), BF16)]


def gradient_scratch(width, inner):
    return [
        pltpu.VMEM((width, inner), F32),
        pltpu.VMEM((KERNEL_TAPS * inner, inner), F32),
        pltpu.VMEM((inner, width), F32),
        pltpu.VMEM((3, 8, width), F32),
        pltpu.VMEM((6, 8, inner), F32),
        pltpu.VMEM((SLOTS, TAIL_ROWS, inner), BF16),
    ]


PARAMS = dict(vmem_limit_bytes=VMEM_LIMIT, fuse_transposed_lhs_in_matmul=True)


def saved_scratch(lead, length, inner, pad):
    return [pltpu.VMEM(lead + (length + (2 * HALO if pad and i == 0 else 0), inner), BF16) for i in range(6)] + [
        pltpu.VMEM(lead + (length, 2), F32)
    ]


def saved_shapes(parts, length, inner):
    return [jax.ShapeDtypeStruct((parts, length, inner), BF16) for _ in range(6)] + [
        jax.ShapeDtypeStruct((parts, length, 2), F32)
    ]


def cost(units, rows, width, inner):
    flops = units * 2 * rows * (2 * width * inner + KERNEL_TAPS * inner * inner)
    return pl.CostEstimate(flops=int(flops), bytes_accessed=int(rows * width * 10), transcendentals=int(rows * width * 2))


def run_forward(spacing, lens, flags, entry, weights, from_own, span, kept=()):
    save = from_own
    parts, length, width = entry.shape
    inner = width // 2
    count = span[1] - span[0]
    here = (count, length, width)
    plain = [pltpu.VMEM((length + 2 * HALO, inner), BF16), pltpu.VMEM((length, inner), BF16)]
    return pl.pallas_call(
        functools.partial(forward_kernel, spacing, from_own, save, span, len(weights), len(kept)),
        in_specs=[SCALARS] * 2 + [ANYWHERE] * (1 + len(weights) + len(kept)),
        out_specs=[ANYWHERE] * (1 + (N_SAVED if save else 0)),
        scratch_shapes=weight_scratch(width, inner)
        + [
            pltpu.VMEM(here, BF16),
            pltpu.VMEM(here, BF16),
            pltpu.VMEM((TILE, width), BF16),
            pltpu.VMEM((TILE, inner), F32),
            pltpu.VMEM((TILE, width), F32),
            pltpu.VMEM((TILE, KERNEL_TAPS * inner), BF16),
            pltpu.SemaphoreType.DMA((N_SEMS,)),
        ]
        + (saved_scratch((count,), length, inner, True) if save else plain),
        out_shape=[jax.ShapeDtypeStruct(entry.shape, BF16)] + (saved_shapes(parts, length, inner) if save else []),
        input_output_aliases={3 + len(weights) + i: i for i in range(len(kept))},
        compiler_params=pltpu.CompilerParams(**PARAMS),
        cost_estimate=cost(1, count * length, width, inner),
        name="forward_block_own" if from_own else "forward_block_other",
    )(lens, flags, entry, *weights, *kept)


def run_middle(spacing, lens, flags, entry, entry_upper, cot, digits, own, other):
    parts, length, width = entry.shape
    inner = width // 2
    shape = jax.ShapeDtypeStruct(entry.shape, BF16)
    return pl.pallas_call(
        functools.partial(middle_kernel, spacing, parts, len(other)),
        in_specs=[SCALARS] * 2 + [ANYWHERE] * 3 + [pl.BlockSpec(memory_space=pltpu.VMEM)] + [ANYWHERE] * (4 + len(other)),
        out_specs=[ANYWHERE] * 6,
        scratch_shapes=weight_scratch(width, inner)
        + transposed_scratch(width, inner)
        + [pltpu.VMEM(entry.shape, BF16)] * 2
        + [pltpu.VMEM((length, width), BF16)]
        + [pltpu.VMEM((length + 2 * HALO, inner), BF16)] * 2
        + saved_scratch((), length, inner, False)[1:]
        + [
            pltpu.VMEM((TILE, width), BF16),
            pltpu.VMEM((TILE, inner), F32),
            pltpu.VMEM((TILE, width), F32),
            pltpu.VMEM((TILE, inner), BF16),
            pltpu.VMEM((TILE, KERNEL_TAPS * inner), BF16),
        ]
        + gradient_scratch(width, inner)
        + [pltpu.SemaphoreType.DMA((N_SEMS,))],
        out_shape=[shape, shape] + packed_shapes(width, inner),
        input_output_aliases={2: 0},
        compiler_params=pltpu.CompilerParams(**PARAMS),
        cost_estimate=cost(3, parts * length, width, inner),
        name="second_block",
    )(lens, flags, entry, entry_upper, cot, digits, *own, *other)


def packed_shapes(width, inner):
    half = (width + KERNEL_TAPS * inner + 2 * inner + TAIL_ROWS) // 2
    chains = [jax.ShapeDtypeStruct((rows, inner), BF16) for rows in (CHAIN_ROWS, half - CHAIN_ROWS)]
    return chains + chains


def run_first_back(spacing, lens, flags, entry, grad_out, digits, own, saved, packed):
    parts, length, width = entry.shape
    inner = width // 2
    return pl.pallas_call(
        functools.partial(first_back_kernel, spacing, parts),
        in_specs=[SCALARS] * 2 + [ANYWHERE] * 2 + [pl.BlockSpec(memory_space=pltpu.VMEM)] + [ANYWHERE] * (4 + N_SAVED + 4),
        out_specs=[ANYWHERE] * 5,
        scratch_shapes=weight_scratch(width, inner)
        + transposed_scratch(width, inner)
        + [pltpu.VMEM(entry.shape, BF16)] * 2
        + [pltpu.VMEM((length, width), BF16)]
        + [pltpu.VMEM((length + 2 * HALO, inner), BF16)]
        + [
            pltpu.VMEM((TILE, width), BF16),
            pltpu.VMEM((TILE, inner), F32),
            pltpu.VMEM((TILE, width), F32),
            pltpu.VMEM((TILE, inner), BF16),
            pltpu.VMEM((TILE, KERNEL_TAPS * inner), BF16),
        ]
        + gradient_scratch(width, inner)
        + saved_scratch((), length, inner, True)[:-1]
        + [pltpu.VMEM((parts, length, 2), F32)]
        + [pltpu.SemaphoreType.DMA((N_SEMS,))],
        out_shape=[jax.ShapeDtypeStruct(entry.shape, BF16)] + [jax.ShapeDtypeStruct(half.shape, BF16) for half in packed],
        input_output_aliases={3: 0, **{9 + N_SAVED + i: 1 + i for i in range(4)}},
        compiler_params=pltpu.CompilerParams(**PARAMS),
        cost_estimate=cost(2, parts * length, width, inner),
        name="first_block_back",
    )(lens, flags, entry, grad_out, digits, *own, *saved, *packed)


def unwritten(like):
    return pl.pallas_call(
        lambda out: None,
        out_specs=ANYWHERE,
        out_shape=jax.ShapeDtypeStruct(like.shape, like.dtype),
        name="unwritten",
    )()


def swap_sections(value):
    return lax.ppermute(value, "section", [(0, 1), (1, 0)])


def swap_dp(value, bit):
    count = lax.axis_size("dp")
    return lax.ppermute(value, "dp", [(i, i ^ bit) for i in range(count)])


RING = (0, 2, 4, 6, 7, 5, 3, 1)
CORE, Y_SIDE, Z_SIDE = 1, 2, 4


def vec_block(vec_d, vec_h):
    inner = vec_h.shape[1]

    def padded(rows, count):
        return jnp.pad(rows, ((0, count - rows.shape[0]), (0, 0)))

    return jnp.concatenate([padded(vec_d[:, :inner], 8), padded(vec_d[:, inner:], 8), padded(vec_h, 16)], 0)


def brought_over(vecs, w_in, w_conv, w_out):
    if lax.axis_size("dp") != 2 * len(RING):
        rest = []
        for weight in (w_in, w_conv, w_out):
            rows = weight.shape[0] // lax.axis_size("dp")
            rest.append(lax.dynamic_slice_in_dim(weight, lax.axis_index("dp") * rows, rows, 0))
        return tuple(swap_sections(value) for value in (vecs, *rest))
    unit = lax.axis_index("dp") & 7
    inner = w_in.shape[1]
    out_part = lax.dynamic_slice_in_dim(w_out, unit * WOUT_PART, WOUT_PART, 0)
    first = jnp.concatenate(
        [lax.dynamic_slice_in_dim(w_in, unit * WIN_PART, WIN_PART, 0), out_part[:, :inner], out_part[:, inner:], vecs], 0
    )
    second = lax.dynamic_slice_in_dim(w_conv, unit * WCONV_PART, WCONV_PART, 0)
    return swap_sections(first), swap_sections(second)


def spread_shares(shares, work, rest):
    done = work()
    shares = lax.optimization_barrier((shares, done))[0]
    if lax.axis_size("dp") != 2 * len(RING):
        gathered = (shares[0], *(lax.all_gather(share, "dp", axis=0, tiled=True) for share in shares[1:]))
        return gathered, rest(done)
    along = [(own, swap_dp(own, CORE), swap_dp(own, Y_SIDE), swap_dp(own, Z_SIDE)) for own in shares]
    done = rest(done)
    along = lax.optimization_barrier((along, done))[0]
    result = []
    for (own, own_crossed, along_y, along_z), relay in zip(along, (True, False)):
        across = swap_dp(along_z, Y_SIDE) if relay else swap_dp(along_y, Z_SIDE)
        result += [own, own_crossed]
        for value in (along_y, along_z, across):
            result += [value, swap_dp(value, CORE)]
    return tuple(result), done


def ring_place():
    chips = len(RING)
    place = jnp.asarray([RING.index(i // 2) for i in range(2 * chips)], jnp.int32)[lax.axis_index("dp")]
    return jnp.where(lax.axis_index("dp") & 1 == 0, place, (chips - place) % chips)


def found_places(count):
    core = lax.axis_index("dp") & 1
    if count == 1:
        where = [jnp.int32(0)] * 2
    else:
        here = ring_place()
        where = [(at + 1 - step) % count for at in (here, (count - here) % count) for step in range(count)]
    halves = [core] * count + [1 - core] * count
    return jnp.stack([jnp.stack(halves), jnp.stack(where)]).astype(jnp.int32)


def ring_sum(mine, theirs):
    core = lax.axis_index("dp") & 1
    if lax.axis_size("dp") != 2 * len(RING):
        halves = []
        for own, other in zip(mine, theirs):
            first, second = jnp.where(core == 0, own, other), jnp.where(core == 0, other, own)
            first, second = lax.psum((first, second), "dp")
            halves.append((jnp.where(core == 0, first, second), jnp.where(core == 0, second, first)))
        return [[half[0]] for half in halves], [[half[1]] for half in halves], [half[0][:8, :128] for half in halves]
    chips = len(RING)
    width = mine[0].shape[1]
    at = ring_place()
    pairs = []
    for p in range(chips):
        after = (p + 1) % chips
        pairs.append((2 * RING[p], 2 * RING[after]))
        pairs.append((2 * RING[after] + 1, 2 * RING[p] + 1))

    def onward(value):
        return lax.ppermute(value, "dp", pairs)

    def pick(values, which):
        return lax.dynamic_index_in_dim(values, which % chips, 0, keepdims=False)

    def put(values, value, which):
        return lax.dynamic_update_slice(values, value[None], (which % chips, 0, 0))

    def plus(left, right):
        return (left.astype(F32) + right.astype(F32)).astype(BF16)

    chains = range(len(mine))
    mine = [value.reshape(chips, -1, width) for value in mine]
    theirs = [swap_dp(value, CORE).reshape(chips, -1, width) for value in theirs]

    def term(i, which):
        return pick(mine[i], which).astype(F32) + pick(theirs[i], which).astype(F32)

    moving = [term(i, at).astype(BF16) for i in chains]
    for step in range(chips - 1):
        moving = [(onward(moving[i]).astype(F32) + term(i, at - step - 1)).astype(BF16) for i in chains]
    found = [[value] for value in moving]
    crossed = [[swap_dp(value, CORE)] for value in moving]
    marks = [value[:8, :128] for value in moving]
    for step in range(1, chips):
        for i in chains:
            arrived = onward(moving[i])
            moving[i], marks[i], crossed[i][-1] = lax.optimization_barrier(
                (arrived, marks[i] + arrived[:8, :128], crossed[i][-1])
            )
            found[i].append(moving[i])
            crossed[i].append(swap_dp(moving[i], CORE))
    return found, crossed, marks


def unpack_kernel(ranges, n_found, n_kept, n_targets, places, *refs):
    found, refs = refs[:n_found], refs[n_found + 1 + n_kept :]
    targets, (tail_out, wide_v, sems) = refs[:n_targets], refs[n_targets:]
    size, width = found[0].shape
    for i, ref in enumerate(found):
        wide_v[places[0, i], pl.ds(pl.multiple_of(places[1, i] * size, 16), size), :] = ref[...].astype(F32)
    stores = Copies(sems)
    for half, first, rows, target, row, column in ranges:
        stores.start(
            wide_v.at[half, first : first + rows], targets[target].at[row : row + rows, column : column + width]
        )
    tail_out[...] = wide_v[0, 0:TAIL_ROWS, :]
    stores.wait()


def unpack(places, found, marks, width, inner):
    shapes = [(width, inner), (KERNEL_TAPS * inner, inner), (inner, width)]
    spans = [(0, width, 0), (1, KERNEL_TAPS * inner, 0), (2, inner, 0), (2, inner, inner)]
    sizes = [sum(value.shape[0] for value in values) // 2 for values in found]
    starts = [(half, chain, half * sum(sizes) + chain * sizes[0], sizes[chain]) for half in range(2) for chain in range(2)]
    outs, tails = (), []
    for chain in range(2):
        ranges = []
        for half, of_chain, start, size in starts:
            at = TAIL_ROWS
            for target, rows, column in spans:
                low, high = max(start, at), min(start + size, at + rows)
                if of_chain == chain and low < high:
                    ranges.append((half, low - start, high - low, target, low - at, column))
                at += rows
        count = len(found[chain])
        *outs, tail = pl.pallas_call(
            functools.partial(unpack_kernel, tuple(ranges), count, len(outs), len(shapes)),
            in_specs=[SCALARS] + [pl.BlockSpec(memory_space=pltpu.VMEM)] * count + [ANYWHERE] * (1 + len(outs)),
            out_specs=[ANYWHERE] * len(shapes) + [pl.BlockSpec(memory_space=pltpu.VMEM)],
            scratch_shapes=[
                pltpu.VMEM((2, sizes[chain], inner), F32),
                pltpu.SemaphoreType.DMA((8,)),
            ],
            out_shape=[jax.ShapeDtypeStruct(shape, F32) for shape in shapes]
            + [jax.ShapeDtypeStruct((TAIL_ROWS, inner), F32)],
            input_output_aliases={2 + count + i: i for i in range(len(outs))},
            compiler_params=pltpu.CompilerParams(vmem_limit_bytes=VMEM_LIMIT // 2),
            name="unpack_chain",
        )(places, *found[chain], marks[chain], *outs)
        tails.append(tail)
    return (*outs, tails[0])


def digit_base():
    base = 2
    while (2 * base - 1) * lax.axis_size("dp") <= 256:
        base *= 2
    return base


def local(tokens, cotangent, lengths, predicted, truth, vec_d, w_in, vec_h, w_conv, w_out):
    section_id = lax.axis_index("section")
    lower = jnp.where(section_id == 0, 1, 0).astype(jnp.int32)
    micro, seq_count, length, width = tokens.shape
    inner = width // 2
    parts = micro * seq_count
    lens = lengths.reshape(parts)
    entry = tokens.reshape(parts, length, width)
    cot = cotangent.reshape(parts, length, width)
    own = (vec_block(vec_d[0], vec_h[0]), w_in[0], w_conv[0], w_out[0])
    shares = brought_over(*own)
    unit = lax.axis_index("dp") & 7

    positions = lax.broadcasted_iota(jnp.int32, predicted.shape, 2) + section_id * predicted.shape[2]
    live_rows = positions < lengths[:, :, None]
    right_rows = live_rows & (predicted == truth)
    kind_hits = truth[..., None] == jnp.arange(TYPES, dtype=jnp.int32)
    correct = jnp.sum((kind_hits & right_rows[..., None]).astype(jnp.int32), (0, 1, 2))
    totals = jnp.sum((kind_hits & live_rows[..., None]).astype(jnp.int32), (0, 1, 2))
    counts = jnp.concatenate([correct, totals])
    base = digit_base()
    n_digits = 1
    while base**n_digits <= parts * length:
        n_digits += 1
    places = jnp.asarray([base**i for i in range(n_digits)], jnp.int32)
    digits = (counts[None, :] // places[:, None]) % base
    digits = jnp.pad(digits.reshape(1, -1).astype(F32), ((0, 15), (0, inner - n_digits * 2 * TYPES)))

    core = lax.axis_index("dp") & 1
    on_lower = jnp.stack([lower, unit, core])
    on_upper = jnp.stack([1 - lower, unit, core])
    middle_part = (parts + 1) // 2
    other, (act, *saved) = spread_shares(
        shares,
        lambda: run_forward(FIRST_DILATION, lens, on_lower, entry, own, True, (0, middle_part)),
        lambda kept: run_forward(FIRST_DILATION, lens, on_lower, entry, own, True, (middle_part, parts), kept),
    )
    act_upper = lax.cond(
        section_id == 1,
        lambda: run_forward(FIRST_DILATION, lens, on_upper, entry, other, False, (0, parts))[0],
        lambda: unwritten(entry),
    )
    acts, grad_middle, *packed = run_middle(SECOND_DILATION, lens, on_upper, act, act_upper, cot, digits, own, other)
    in_grads, *packed = run_first_back(FIRST_DILATION, lens, on_lower, entry, grad_middle, digits, own, saved, packed)
    found, crossed, marks = ring_sum(packed[:2], packed[2:])
    found = [left + right for left, right in zip(found, crossed)]
    g_in, g_conv, g_out, tail = unpack(found_places(len(found[0]) // 2), found, marks, width, inner)
    digit_sums = tail[32, : n_digits * 2 * TYPES]
    digit_sums = (digit_sums + swap_sections(digit_sums)).astype(jnp.int32).reshape(n_digits, 2 * TYPES)
    return (
        acts.reshape(tokens.shape)[None],
        in_grads.reshape(tokens.shape)[None],
        jnp.concatenate([tail[0:3], tail[8:11]], 1)[None],
        g_in[None],
        tail[16:22][None],
        g_conv[None],
        g_out[None],
        jnp.sum(digit_sums * places[:, None], 0).reshape(2, TYPES),
    )


def solution(mesh):
    return jax.shard_map(
        local,
        mesh=mesh,
        in_specs=(
            P(None, "dp", None, None),
            P(None, "dp", None, None),
            P(None, "dp"),
            P(None, "dp", "section"),
            P(None, "dp", "section"),
            P("section", None, None),
            P("section", None, None),
            P("section", None, None),
            P("section", None, None),
            P("section", None, None),
        ),
        out_specs=(
            P("section", None, "dp", None, None),
            P("section", None, "dp", None, None),
            P("section", None, None),
            P("section", None, None),
            P("section", None, None),
            P("section", None, None),
            P("section", None, None),
            P(),
        ),
        check_vma=False,
    )
```
